32 devices in a mesh: dp: 4 (over y, core), shard: 8 (over z, x).
Axes of the slice: x: 2, y: 2, z: 4, core: 2. Of those that a mesh axis runs over, the one named last changes fastest.
Arguments:
- grads: bfloat16 [4, 18, 7168, 128], P('dp', None, 'shard'), may hold values from -230 to 230
- params: float32 [18, 7168, 128], P(None, 'shard'), may hold values from -6 to 6
- table: int32 [18], replicated, may hold values from 0 to 17, each once
Outputs:
- new_params: float32 [18, 7168, 128], P(None, 'shard')
- update: bfloat16 [18, 7168, 128], P(None, 'shard')
The draws below stay inside these ranges and needn't reach their ends.
Inputs may be any that keep to these rules, and one draw needn't show every extreme that they name: A permutation: gradient block j belongs to head table[j].
All inputs are finite; a program needn't handle non-finite values.
Results may differ from the reference program's by a relative error of at most 0.006.
Values may be sent and summed in bfloat16 or wider, within the bound.
No kernel may reach another device: no remote copies, remote signals or barrier semaphores. Data moves between devices by JAX's collectives and lax.ppermute only.
A program may use at most 128 MiB of HBM per device.

```python
import math
import jax
import jax.numpy as jnp
from jax import lax

D = 7168
V = 128
NMAT = 18
ITERS = 5
N_DP = 4


def draw_grads(key, part):
    key = jax.random.fold_in(key, 5)
    keys = jax.random.split(key, 3)
    shape = (N_DP, NMAT, D, V)
    base = jnp.clip(jax.random.normal(keys[0], shape, jnp.float32), -5.0, 5.0)
    row_scale = jnp.exp(jax.random.uniform(keys[1], (1, NMAT, D, 1), jnp.float32, 0.0, math.log(10.0)))
    row_rise = jnp.exp(math.log(3.0) * jnp.arange(D, dtype=jnp.float32) / D).reshape(1, 1, D, 1)
    col_scale = jnp.exp(jax.random.uniform(keys[2], (1, 1 * NMAT, 1, V), jnp.float32, 0.0, math.log(10.0)))
    replica_rise = jnp.exp(math.log(3.0) * jnp.arange(N_DP, dtype=jnp.float32) / max(N_DP - 1, 1)).reshape(N_DP, 1, 1, 1)
    values = 0.05 * base * row_scale * row_rise * col_scale * replica_rise
    return values.astype(jnp.bfloat16)


def level_of(own_key, dims, cuts, smallest, high):
    def one(position, shards_of):
        heights = jax.random.uniform(jax.random.fold_in(jax.random.fold_in(own_key, 6), position), (shards_of,), jnp.float32, smallest / len(cuts), high / len(cuts))
        return jnp.repeat(jnp.exp(heights), dims[position] // shards_of).reshape((-1,) + (1,) * (len(dims) - position - 1))

    factor_of = one(*cuts[0])
    for cut in cuts[1:]:
        factor_of = factor_of * one(*cut)
    return factor_of


def gaussian(key, shape, scale, bound, cuts=(), kind=jnp.bfloat16):
    result = scale * jax.random.normal(key, shape, jnp.float32)
    if cuts:
        result = result * level_of(key, shape, cuts, -0.22, 0.18)
    return jnp.clip(result, -bound, bound).astype(kind)


def setup_inputs(seed: int = 0) -> dict:
    streams_of = jax.random.split(jax.random.key(seed), 4)
    return {
        "grads": draw_grads(jax.random.fold_in(streams_of[3], 71), 0),
        "params": gaussian(streams_of[1], (NMAT, D, V), 1.0, 6.0, ((1, 8),), jnp.float32),
        "table": jax.random.permutation(streams_of[2], NMAT).astype(jnp.int32),
    }


quintic_one = 3.4445
quintic_two = -4.775
quintic_three = 2.0315
epsilon = 1e-07
learning_rate = 0.02
decay_rate = 0.1

def orthogonal_one(block):
    wide = block.astype(jnp.float32)
    norm_value = jnp.sqrt(jnp.sum(wide * wide))
    current = wide / (norm_value + epsilon)
    for index in range(ITERS):
        gram = jnp.dot(current.T, current, precision=lax.Precision.HIGHEST, preferred_element_type=jnp.float32)
        poly = quintic_two * gram + quintic_three * jnp.dot(gram, gram, precision=lax.Precision.HIGHEST, preferred_element_type=jnp.float32)
        current = quintic_one * current + jnp.dot(current, poly, precision=lax.Precision.HIGHEST, preferred_element_type=jnp.float32)
    return current.astype(jnp.bfloat16)

def reference(grads, params, table):
    total = jnp.zeros(grads.shape[1:], jnp.float32)
    for index in range(N_DP):
        total = total + grads[index].astype(jnp.float32)
    blocks = total.astype(jnp.bfloat16)
    ortho = lax.map(orthogonal_one, blocks)
    heads = jnp.zeros_like(ortho).at[table].set(ortho)
    scaled = 0.2 * math.sqrt(max(D, V)) * heads.astype(jnp.float32)
    new_params = params - learning_rate * (scaled + decay_rate * params)
    return (new_params, scaled.astype(jnp.bfloat16))
```

```python
import functools
import math

import jax
import jax.numpy as jnp
from jax import lax
from jax.experimental import pallas as pl
from jax.experimental.pallas import tpu as pltpu
from jax.sharding import PartitionSpec as P

D = 7168
V = 128
ITERS = 5
CORES = 2

quintic_one = 3.4445
quintic_two = -4.775
quintic_three = 2.0315
epsilon = 1e-07
learning_rate = 0.02
decay_rate = 0.1
HIGHEST = lax.Precision.HIGHEST


def dot32(left, right):
    return jnp.dot(left, right, precision=HIGHEST, preferred_element_type=jnp.float32)


def newton_kernel(parts_ref, out_ref):
    gram = parts_ref[0, 0]
    for index in range(1, parts_ref.shape[0]):
        gram = gram + parts_ref[index, 0]
    rows = lax.broadcasted_iota(jnp.int32, (V, V), 0)
    columns = lax.broadcasted_iota(jnp.int32, (V, V), 1)
    eye = (rows == columns).astype(jnp.float32)
    norm_value = jnp.sqrt(jnp.sum(gram * eye))
    scale = 1.0 / (norm_value + epsilon)
    gram = (gram * scale) * scale
    product = None
    for index in range(ITERS):
        poly = quintic_one * eye + quintic_two * gram + quintic_three * dot32(gram, gram)
        product = poly if product is None else dot32(product, poly)
        if index < ITERS - 1:
            gram = dot32(dot32(gram, poly), poly)
    out_ref[0] = product * scale


def newton_schulz(parts):
    groups, items = parts.shape[:2]
    return pl.pallas_call(
        newton_kernel,
        out_shape=jax.ShapeDtypeStruct((items, V, V), jnp.float32),
        grid=(items,),
        in_specs=[pl.BlockSpec((groups, 1, V, V), lambda i: (0, i, 0, 0))],
        out_specs=pl.BlockSpec((1, V, V), lambda i: (i, 0, 0)),
        cost_estimate=pl.CostEstimate(
            flops=items * 18 * 12 * V**3, bytes_accessed=groups * items * V * V * 4, transcendentals=0
        ),
    )(parts)


def apply_kernel(starts, heads_ref, picks_ref, *refs):
    count = len(starts) - 1
    sources = refs[:count]
    q_ref, params_ref, new_ref, update_ref = refs[count:]
    step = pl.program_id(0)
    q = q_ref[0]
    high = q.astype(jnp.bfloat16)
    low = (q - high.astype(jnp.float32)).astype(jnp.bfloat16)

    def work(source):
        rows = source[0]
        ortho = jnp.dot(rows, high, preferred_element_type=jnp.float32)
        ortho = ortho + jnp.dot(rows, low, preferred_element_type=jnp.float32)
        ortho = ortho.astype(jnp.bfloat16).astype(jnp.float32)
        scaled = 0.2 * math.sqrt(max(D, V)) * ortho
        params = params_ref[0]
        new_ref[0] = params - learning_rate * (scaled + decay_rate * params)
        update_ref[0] = scaled.astype(jnp.bfloat16)

    for index, source in enumerate(sources):
        if count == 1:
            work(source)
        else:
            inside = (step >= starts[index]) & (step < starts[index + 1])
            pl.when(inside)(functools.partial(work, source))


def apply_all(sources, q, params, heads, picks):
    count, rows, width = params.shape
    starts = [0]
    for source in sources:
        starts.append(starts[-1] + source.shape[0])
    assert starts[-1] == count

    def source_map(start, items, i, heads_ref, picks_ref):
        return (jnp.clip(i - start, 0, items - 1), 0, 0)

    def head_map(i, heads_ref, picks_ref):
        return (heads_ref[i], 0, 0)

    source_specs = [
        pl.BlockSpec((1, rows, width), functools.partial(source_map, start, source.shape[0]))
        for start, source in zip(starts, sources)
    ]
    grid_spec = pltpu.PrefetchScalarGridSpec(
        num_scalar_prefetch=2,
        grid=(count,),
        in_specs=source_specs
        + [
            pl.BlockSpec((1, V, V), lambda i, heads_ref, picks_ref: (picks_ref[i], 0, 0)),
            pl.BlockSpec((1, rows, width), head_map),
        ],
        out_specs=[pl.BlockSpec((1, rows, width), head_map)] * 2,
    )
    size = count * rows * width
    return pl.pallas_call(
        functools.partial(apply_kernel, tuple(starts)),
        grid_spec=grid_spec,
        out_shape=[
            jax.ShapeDtypeStruct(params.shape, jnp.float32),
            jax.ShapeDtypeStruct(params.shape, jnp.bfloat16),
        ],
        cost_estimate=pl.CostEstimate(flops=4 * size * V, bytes_accessed=12 * size, transcendentals=0),
        compiler_params=pltpu.CompilerParams(vmem_limit_bytes=32 * 1024 * 1024),
    )(heads, picks, *sources, q, params)


def per_device(grads, params, table):
    local = grads[0]
    count, rows, width = local.shape
    replicas = lax.axis_size("dp")
    groups = lax.axis_size("shard")
    members = replicas // CORES
    own = -(-count // members)
    half = own // CORES
    odd = own % CORES
    place = lax.axis_index("dp")
    core = place % CORES
    member = place // CORES
    if members * own > count:
        filler = jnp.zeros((members * own - count, rows, width), local.dtype)
        local = jnp.concatenate([local, filler], axis=0)

    def pairs_of(shift):
        return [
            (m * CORES + c, ((m + shift) % members) * CORES + c)
            for m in range(members)
            for c in range(CORES)
        ]

    core_pairs = [(m * CORES + c, m * CORES + 1 - c) for m in range(members) for c in range(CORES)]
    odd_pairs = [(m * CORES + 1, m * CORES) for m in range(members)]

    def owned_by(array, owner):
        return lax.dynamic_slice_in_dim(array, owner * own, own, axis=0)

    raws = [owned_by(local, member)]
    for shift in range(1, members):
        outgoing = owned_by(local, (member + shift) % members)
        raws.append(lax.ppermute(outgoing, "dp", pairs_of(shift)))

    def of_core(array, which):
        return lax.dynamic_slice_in_dim(array, which * half, half, axis=0)

    mains, odds = [], []
    for raw in raws:
        arrived = lax.ppermute(of_core(raw, 1 - core), "dp", core_pairs)
        mains.append(of_core(raw, core).astype(jnp.float32) + arrived.astype(jnp.float32))
        if odd:
            last = raw[own - 1 :]
            arrived = lax.ppermute(last, "dp", odd_pairs)
            odds.append(last.astype(jnp.float32) + arrived.astype(jnp.float32))
    main = functools.reduce(jnp.add, mains).astype(jnp.bfloat16)
    pieces = [main]
    if odd:
        extra = functools.reduce(jnp.add, odds).astype(jnp.bfloat16)
        pieces.append(extra)

    gram = jnp.concatenate(
        [
            jnp.einsum("mrv,mrw->mvw", piece, piece, preferred_element_type=jnp.float32)
            for piece in pieces
        ],
        axis=0,
    )
    slots = half + odd
    items = -(-slots // groups)
    gram = jnp.concatenate([gram, jnp.zeros((items * groups - slots, V, V), jnp.float32)], axis=0)
    gram = gram.reshape(groups, items, V, V)
    parts = lax.all_to_all(gram, "shard", split_axis=0, concat_axis=0, tiled=True)
    solved = newton_schulz(parts)
    q_core = lax.all_gather(solved, "shard", axis=0, tiled=True)[:slots]

    def spread(array):
        return [array] + [lax.ppermute(array, "dp", pairs_of(shift)) for shift in range(1, members)]

    main_all = spread(main)
    main_other = [lax.ppermute(array, "dp", core_pairs) for array in main_all]
    extra_all = []
    if odd:
        down_pairs = [(m * CORES, m * CORES + 1) for m in range(members)]
        extra_all = [extra]
        for shift in range(1, members):
            pairs = [pair for pair in pairs_of(shift) if pair[0] % CORES == 0]
            extra_all.append(lax.ppermute(extra, "dp", pairs))
        extra_all = [
            jnp.where(core == 0, array, lax.ppermute(array, "dp", down_pairs)) for array in extra_all
        ]
    q_all = spread(q_core)
    q_other = [lax.ppermute(array, "dp", core_pairs) for array in q_all]

    sources, blocks, qs = [], [], []
    for shift in range(members):
        owner = (member - shift) % members
        for which, array in ((core, main_all[shift]), (1 - core, main_other[shift])):
            sources.append(array)
            blocks.append(owner * own + which * half + jnp.arange(half, dtype=jnp.int32))
        qs.append(q_all[shift][:half])
        qs.append(q_other[shift][:half])
        if odd:
            sources.append(extra_all[shift])
            blocks.append((owner * own + own - 1)[None])
            qs.append(jnp.where(core == 0, q_all[shift][half:], q_other[shift][half:]))
    blocks = jnp.concatenate(blocks).astype(jnp.int32)
    q = jnp.concatenate(qs, axis=0)
    picks = jnp.arange(count, dtype=jnp.int32)
    if members * own > count:
        order = jnp.argsort(blocks)[:count]
        sources = [jnp.concatenate(sources, axis=0)[order]]
        blocks = blocks[order]
        picks = order.astype(jnp.int32)
    heads = table[blocks]
    new_params, update = apply_all(sources, q, params, heads, picks)
    return (new_params, update)


def solution(mesh):
    return jax.shard_map(
        per_device,
        mesh=mesh,
        in_specs=(P("dp", None, "shard", None), P(None, "shard", None), P()),
        out_specs=(P(None, "shard", None), P(None, "shard", None)),
        check_vma=False,
    )
```

```python
import functools
import math

import jax
import jax.numpy as jnp
from jax import lax
from jax.experimental import pallas as pl
from jax.experimental.pallas import tpu as pltpu
from jax.sharding import PartitionSpec as P

D = 7168
V = 128
ITERS = 5
CORES = 2

quintic_one = 3.4445
quintic_two = -4.775
quintic_three = 2.0315
epsilon = 1e-07
learning_rate = 0.02
decay_rate = 0.1
HIGHEST = lax.Precision.HIGHEST


def dot32(left, right):
    return jnp.dot(left, right, precision=HIGHEST, preferred_element_type=jnp.float32)


def newton_kernel(gram_ref, out_ref):
    items = gram_ref.shape[0]
    rows = lax.broadcasted_iota(jnp.int32, (V, V), 0)
    columns = lax.broadcasted_iota(jnp.int32, (V, V), 1)
    eye = (rows == columns).astype(jnp.float32)
    grams, scales = [], []
    for item in range(items):
        gram = gram_ref[item]
        norm_value = jnp.sqrt(jnp.sum(gram * eye))
        scale = 1.0 / (norm_value + epsilon)
        scales.append(scale)
        grams.append((gram * scale) * scale)
    products = [None] * items
    for index in range(ITERS):
        squares = [dot32(gram, gram) for gram in grams]
        polys = [
            quintic_one * eye + quintic_two * gram + quintic_three * square
            for gram, square in zip(grams, squares)
        ]
        if index < ITERS - 1:
            halves = [dot32(gram, poly) for gram, poly in zip(grams, polys)]
        if index == 0:
            products = polys
        else:
            products = [dot32(product, poly) for product, poly in zip(products, polys)]
        if index < ITERS - 1:
            grams = [dot32(half, poly) for half, poly in zip(halves, polys)]
    for item in range(items):
        out_ref[item] = products[item] * scales[item]


def newton_schulz(gram):
    items = gram.shape[0]
    return pl.pallas_call(
        newton_kernel,
        out_shape=jax.ShapeDtypeStruct((items, V, V), jnp.float32),
        in_specs=[pl.BlockSpec(memory_space=pltpu.VMEM)],
        out_specs=pl.BlockSpec(memory_space=pltpu.VMEM),
        cost_estimate=pl.CostEstimate(
            flops=items * 18 * 12 * V**3, bytes_accessed=items * V * V * 8, transcendentals=0
        ),
        compiler_params=pltpu.CompilerParams(vmem_limit_bytes=16 * 1024 * 1024),
    )(gram)


def apply_kernel(starts, heads_ref, places_ref, picks_ref, valid_ref, *refs):
    count = len(starts) - 1
    sources = refs[:count]
    q_ref, params_ref = refs[count : count + 2]
    new_ref, update_ref = refs[-2:]
    step = pl.program_id(0)

    def work(source):
        q = q_ref[0]
        high = q.astype(jnp.bfloat16)
        low = (q - high.astype(jnp.float32)).astype(jnp.bfloat16)
        rows = source[0]
        ortho = jnp.dot(rows, high, preferred_element_type=jnp.float32)
        ortho = ortho + jnp.dot(rows, low, preferred_element_type=jnp.float32)
        ortho = ortho.astype(jnp.bfloat16).astype(jnp.float32)
        scaled = 0.2 * math.sqrt(max(D, V)) * ortho
        params = params_ref[0]
        new_ref[0] = params - learning_rate * (scaled + decay_rate * params)
        update_ref[0] = scaled.astype(jnp.bfloat16)

    for index, source in enumerate(sources):
        inside = (step >= starts[index]) & (step < starts[index + 1]) & (valid_ref[step] > 0)
        pl.when(inside)(functools.partial(work, source))


def apply_chunk(sources, q, params, previous, heads, places, picks, valid):
    count, rows, width = params.shape
    unit = sources[0].shape[1]
    starts = [0]
    for source in sources:
        starts.append(starts[-1] + source.shape[0])

    def source_map(start, items, i, *refs):
        return (jnp.clip(i - start, 0, items - 1), 0, 0)

    def head_map(i, heads_ref, places_ref, picks_ref, valid_ref):
        return (heads_ref[i], places_ref[i], 0)

    def pick_map(i, heads_ref, places_ref, picks_ref, valid_ref):
        return (picks_ref[i], 0, 0)

    in_specs = [
        pl.BlockSpec((1, unit, width), functools.partial(source_map, start, source.shape[0]))
        for start, source in zip(starts, sources)
    ]
    in_specs.append(pl.BlockSpec((1, V, V), pick_map))
    in_specs.append(pl.BlockSpec((1, unit, width), head_map))
    operands = [heads, places, picks, valid, *sources, q, params]
    aliases = {}
    for index, array in enumerate(previous):
        aliases[len(operands)] = index
        operands.append(array)
        in_specs.append(pl.BlockSpec(memory_space=pl.ANY))
    size = starts[-1] * unit * width
    return pl.pallas_call(
        functools.partial(apply_kernel, tuple(starts)),
        grid_spec=pltpu.PrefetchScalarGridSpec(
            num_scalar_prefetch=4,
            grid=(starts[-1],),
            in_specs=in_specs,
            out_specs=[pl.BlockSpec((1, unit, width), head_map)] * 2,
        ),
        out_shape=[
            jax.ShapeDtypeStruct(params.shape, jnp.float32),
            jax.ShapeDtypeStruct(params.shape, jnp.bfloat16),
        ],
        input_output_aliases=aliases,
        cost_estimate=pl.CostEstimate(flops=4 * size * V, bytes_accessed=12 * size, transcendentals=0),
        compiler_params=pltpu.CompilerParams(vmem_limit_bytes=16 * 1024 * 1024),
    )(*operands)


def chunk_sizes(own):
    if own <= 3:
        return [own]
    first = 3 if own % 2 else 2
    rest = own - first
    last = 2 if rest > 2 else 0
    return [size for size in (first, rest - last, last) if size]


def swap(array, axis, distance):
    size = lax.axis_size(axis)
    return lax.ppermute(array, axis, [(i, i ^ distance) for i in range(size)])


def gram_of(rows_array, rows):
    blocks = rows_array.reshape(-1, rows, V)
    return jnp.einsum("mrv,mrw->mvw", blocks, blocks, preferred_element_type=jnp.float32)


def per_device(grads, params, table):
    local = grads[0]
    count, rows, width = local.shape
    replicas = lax.axis_size("dp")
    groups = lax.axis_size("shard")
    members = replicas // CORES
    own = -(-count // members)
    place = lax.axis_index("dp")
    core = place % CORES
    member = place // CORES
    if members * own > count:
        filler = jnp.zeros((members * own - count, rows, width), local.dtype)
        local = jnp.concatenate([local, filler], axis=0)
    flat = local.reshape(members * own * rows, width)

    sizes = chunk_sizes(own)
    offsets = [sum(sizes[:k]) for k in range(len(sizes))]

    sums = []
    for size, offset in zip(sizes, offsets):
        share = size * rows // CORES

        def part_of(index):
            start = ((index // CORES) * own + offset) * rows + (index % CORES) * share
            return lax.dynamic_slice_in_dim(flat, start, share, axis=0)

        terms = [part_of(place)]
        for distance in range(1, replicas):
            terms.append(swap(part_of(place ^ distance), "dp", distance))
        terms = [term.astype(jnp.float32) for term in terms]
        while len(terms) > 1:
            terms = [left + right for left, right in zip(terms[::2], terms[1::2])]
        sums.append(terms[0].astype(jnp.bfloat16))

    qs = []
    for size, total in zip(sizes, sums):
        if size % 2:
            whole = size // 2
            half = lax.dynamic_slice_in_dim(total, (1 - core) * whole * rows, rows // 2, axis=0)
            gram = gram_of(half, rows // 2)
            gram = gram + swap(gram, "dp", 1)
            if whole:
                full = lax.dynamic_slice_in_dim(total, core * (rows // 2), whole * rows, axis=0)
                gram = jnp.concatenate([gram_of(full, rows), gram], axis=0)
        else:
            gram = gram_of(total, rows)
        distance = 1
        while distance < groups:
            gram = gram + swap(gram, "shard", distance)
            distance *= 2
        qs.append(newton_schulz(gram))

    def spread(array):
        result = []
        for distance in range(members):
            mine = swap(array, "dp", distance * CORES) if distance else array
            result.append(mine)
            result.append(swap(mine, "dp", 1))
        return result

    outputs = []
    for size, offset, total, q in zip(sizes, offsets, sums, qs):
        per_block = 2 if size % 2 else 1
        units = size * per_block // CORES
        sources = [array.reshape(units, rows // per_block, width) for array in spread(total)]
        q_all = jnp.concatenate(spread(q), axis=0)
        slots = q.shape[0]
        shape = (members, CORES, units)
        distance = lax.broadcasted_iota(jnp.int32, shape, 0)
        other = lax.broadcasted_iota(jnp.int32, shape, 1)
        unit = lax.broadcasted_iota(jnp.int32, shape, 2)
        holder = core ^ other
        within = holder * units + unit
        block = within // per_block
        places = (within % per_block).reshape(-1)
        slot = block - holder * slots
        if size % 2:
            slot = jnp.where(block == size // 2, slots - 1, slot)
        picks = ((distance * CORES + other) * slots + slot).reshape(-1)
        block = ((member ^ distance) * own + offset + block).reshape(-1)
        valid = block < count
        heads = table[jnp.minimum(block, count - 1)]
        if members * own > count:
            order = jnp.arange(valid.shape[0], dtype=jnp.int32)
            latest = lax.cummax(jnp.where(valid, order, -1))
            latest = jnp.where(latest < 0, jnp.argmax(valid).astype(jnp.int32), latest)
            heads, places = heads[latest], places[latest]
        outputs = apply_chunk(
            sources, q_all, params, outputs, heads, places, picks, valid.astype(jnp.int32)
        )
    new_params, update = outputs
    return (new_params, update)


def solution(mesh):
    return jax.shard_map(
        per_device,
        mesh=mesh,
        in_specs=(P("dp", None, "shard", None), P(None, "shard", None), P()),
        out_specs=(P(None, "shard", None), P(None, "shard", None)),
        check_vma=False,
    )
```

```python
import functools
import math

import jax
import jax.numpy as jnp
from jax import lax
from jax.experimental import pallas as pl
from jax.experimental.pallas import tpu as pltpu
from jax.sharding import PartitionSpec as P

D = 7168
V = 128
ITERS = 5
CORES = 2

quintic_one = 3.4445
quintic_two = -4.775
quintic_three = 2.0315
epsilon = 1e-07
learning_rate = 0.02
decay_rate = 0.1
HIGHEST = lax.Precision.HIGHEST


def dot32(left, right):
    return jnp.dot(left, right, precision=HIGHEST, preferred_element_type=jnp.float32)


def newton_kernel(gram_ref, arrived_ref, *refs):
    *earlier, out_ref = refs
    skip = 0
    for ref in earlier:
        out_ref[: ref.shape[0]] = ref[...]
        skip = ref.shape[0]
    items = gram_ref.shape[0]
    rows = lax.broadcasted_iota(jnp.int32, (V, V), 0)
    columns = lax.broadcasted_iota(jnp.int32, (V, V), 1)
    eye = (rows == columns).astype(jnp.float32)
    grams, scales = [], []
    for item in range(items):
        gram = gram_ref[item] + arrived_ref[item]
        norm_value = jnp.sqrt(jnp.sum(gram * eye))
        scale = 1.0 / (norm_value + epsilon)
        scales.append(scale)
        grams.append((gram * scale) * scale)
    products = [None] * items
    for index in range(ITERS):
        squares = [dot32(gram, gram) for gram in grams]
        polys = [
            quintic_one * eye + quintic_two * gram + quintic_three * square
            for gram, square in zip(grams, squares)
        ]
        if index < ITERS - 1:
            halves = [dot32(gram, poly) for gram, poly in zip(grams, polys)]
        if index == 0:
            products = polys
        else:
            products = [dot32(product, poly) for product, poly in zip(products, polys)]
        if index < ITERS - 1:
            grams = [dot32(half, poly) for half, poly in zip(halves, polys)]
    for item in range(items):
        out_ref[skip + item] = products[item] * scales[item]


def newton_schulz(gram, arrived, *earlier):
    items = gram.shape[0]
    slots = items + sum(q.shape[0] for q in earlier)
    return pl.pallas_call(
        newton_kernel,
        out_shape=jax.ShapeDtypeStruct((slots, V, V), jnp.float32),
        in_specs=[pl.BlockSpec(memory_space=pltpu.VMEM)] * (2 + len(earlier)),
        out_specs=pl.BlockSpec(memory_space=pltpu.VMEM),
        cost_estimate=pl.CostEstimate(
            flops=items * 18 * 12 * V**3, bytes_accessed=items * V * V * 12, transcendentals=0
        ),
        compiler_params=pltpu.CompilerParams(vmem_limit_bytes=16 * 1024 * 1024),
    )(gram, arrived, *earlier)


def apply_kernel(layout, place_ref, table_ref, *refs):
    count, first, base, size, offset, own, total, padded = layout
    sources, qs = refs[:count], refs[count : 2 * count]
    params_ref = refs[2 * count]
    new_ref, update_ref, new_buf, update_buf, new_sems, update_sems = refs[-6:]
    per_block = 2 if size % 2 else 1
    units, unit_rows = sources[0].shape[:2]
    whole = size // 2
    place = place_ref[0]

    def locate(source, unit):
        holder = (place ^ source) & (CORES - 1)
        within = holder * units + unit
        block = within >> (per_block - 1)
        index = ((place ^ source) >> (CORES - 1)) * own + offset + block
        head = table_ref[jnp.minimum(index, total - 1) if padded else index]
        start = pl.multiple_of((within & (per_block - 1)) * unit_rows, unit_rows)
        slot = unit
        if per_block > 1:
            slot = jnp.where(block == whole, whole, block - holder * (whole + 1))
        return index < total, head, pl.ds(start, unit_rows), base + slot

    items = [
        (index, unit, index * units + unit, locate(first + index, unit))
        for index in range(count)
        for unit in range(units)
    ]

    def compute(index, unit, item, head, span, slot):
        q = qs[index][slot]
        high = q.astype(jnp.bfloat16)
        low = (q - high.astype(jnp.float32)).astype(jnp.bfloat16)
        rows = sources[index][unit]
        ortho = jnp.dot(
            jnp.concatenate([rows, rows], axis=1),
            jnp.concatenate([high, low], axis=0),
            preferred_element_type=jnp.float32,
        )
        ortho = ortho.astype(jnp.bfloat16).astype(jnp.float32)
        scaled = 0.2 * math.sqrt(max(D, V)) * ortho
        params = params_ref[head, span]
        new_buf[item] = params - learning_rate * (scaled + decay_rate * params)
        update_buf[item] = scaled.astype(jnp.bfloat16)
        pltpu.make_async_copy(new_buf.at[item], new_ref.at[head, span], new_sems.at[item]).start()
        pltpu.make_async_copy(
            update_buf.at[item], update_ref.at[head, span], update_sems.at[item]
        ).start()

    def finish(item):
        span = pl.ds(0, unit_rows)
        pltpu.make_async_copy(new_buf.at[item], new_ref.at[0, span], new_sems.at[item]).wait()
        pltpu.make_async_copy(
            update_buf.at[item], update_ref.at[0, span], update_sems.at[item]
        ).wait()

    for index, unit, item, (valid, head, span, slot) in items:
        run = functools.partial(compute, index, unit, item, head, span, slot)
        pl.when(valid)(run) if padded else run()
    for index, unit, item, (valid, head, span, slot) in items:
        run = functools.partial(finish, item)
        pl.when(valid)(run) if padded else run()


def apply_side(sources, qs, params, previous, place, table, first, base, size, offset, own, padded):
    total, rows, width = params.shape
    count = len(sources)
    units, unit_rows = sources[0].shape[:2]
    steps = count * units
    vmem = pl.BlockSpec(memory_space=pltpu.VMEM)
    hbm = pl.BlockSpec(memory_space=pltpu.HBM)
    smem = pl.BlockSpec(memory_space=pltpu.SMEM)
    operands = [place, table, *sources, *qs, params]
    in_specs = [smem, smem] + [vmem] * (2 * count + 1)
    aliases = {}
    for index, array in enumerate(previous):
        aliases[len(operands)] = index
        operands.append(array)
        in_specs.append(hbm)
    work = steps * unit_rows * width
    layout = (count, first, base, size, offset, own, total, padded)
    return pl.pallas_call(
        functools.partial(apply_kernel, layout),
        in_specs=in_specs,
        out_specs=[hbm, hbm],
        out_shape=[
            jax.ShapeDtypeStruct(params.shape, jnp.float32),
            jax.ShapeDtypeStruct(params.shape, jnp.bfloat16),
        ],
        scratch_shapes=[
            pltpu.VMEM((steps, unit_rows, width), jnp.float32),
            pltpu.VMEM((steps, unit_rows, width), jnp.bfloat16),
            pltpu.SemaphoreType.DMA((steps,)),
            pltpu.SemaphoreType.DMA((steps,)),
        ],
        input_output_aliases=aliases,
        cost_estimate=pl.CostEstimate(flops=4 * work * V, bytes_accessed=12 * work, transcendentals=0),
        compiler_params=pltpu.CompilerParams(vmem_limit_bytes=24 * 1024 * 1024),
    )(*operands)


def chunk_sizes(own):
    if own <= 4:
        return [own]
    return [own - 4, 4]


def swap(array, axis, distance):
    size = lax.axis_size(axis)
    return lax.ppermute(array, axis, [(i, i ^ distance) for i in range(size)])


def gram_of(rows_array, rows):
    blocks = rows_array.reshape(-1, rows, V)
    return jnp.einsum("mrv,mrw->mvw", blocks, blocks, preferred_element_type=jnp.float32)


def per_device(grads, params, table):
    local = grads[0]
    count, rows, width = local.shape
    replicas = lax.axis_size("dp")
    groups = lax.axis_size("shard")
    members = replicas // CORES
    own = -(-count // members)
    padded = members * own > count
    place = lax.axis_index("dp").astype(jnp.int32)
    core = place % CORES
    member = place // CORES
    if padded:
        filler = jnp.zeros((members * own - count, rows, width), local.dtype)
        local = jnp.concatenate([local, filler], axis=0)
    flat = local.reshape(members * own * rows, width)
    sizes = chunk_sizes(own)

    def rows_of(chip, offset, which, length):
        return lax.dynamic_slice_in_dim(flat, (chip * own + offset) * rows + which * length, length)

    def total_of(terms):
        terms = [term.astype(jnp.float32) for term in terms]
        while len(terms) > 1:
            terms = [sum(terms[i : i + 2][1:], terms[i]) for i in range(0, len(terms), 2)]
        return terms[0]

    def reduce_gram(gram, distance=1):
        while True:
            arrived = swap(gram, "shard", distance)
            distance *= 2
            if distance >= groups:
                return gram, arrived
            gram = gram + arrived

    def over_chips(array):
        return [swap(array, "dp", distance * CORES) for distance in range(1, members)]

    def over_cores(array):
        return [array, swap(array, "dp", 1)]

    def pieces_of(offset, size):
        share = size * rows // CORES
        return [
            rows_of((place ^ distance) // CORES, offset, (place ^ distance) % CORES, share)
            for distance in range(replicas)
        ]

    def exchange(pieces):
        return [swap(piece, "dp", d) if d else piece for d, piece in enumerate(pieces)]

    size = sizes[0]
    terms = exchange(pieces_of(0, size))
    seconds = []
    if len(sizes) > 1:
        pieces = pieces_of(size, sizes[1])
        terms[-1], *pieces = lax.optimization_barrier((terms[-1], *pieces))
        *seconds, late = exchange(pieces)

    first = total_of(terms).astype(jnp.bfloat16)
    whole = size // 2
    if size % 2:
        half = lax.dynamic_slice_in_dim(first, (1 - core) * whole * rows, rows // 2)
        gram = gram_of(half, rows // 2)
        if seconds:
            *seconds, gram = lax.optimization_barrier((*seconds, gram))
        gram = gram + swap(gram, "dp", 1)
        if whole:
            full = lax.dynamic_slice_in_dim(first, core * (rows // 2), whole * rows)
            gram = jnp.concatenate([gram_of(full, rows), gram], axis=0)
    else:
        gram = gram_of(first, rows)
    totals, qs = [first], []
    if seconds:
        gram = gram + swap(gram, "shard", 1)
        late, gram = lax.optimization_barrier((late, gram))
        gram = gram + swap(gram, "shard", 2)
        second = total_of([*seconds, late]).astype(jnp.bfloat16)
        totals.append(second)
        gram_second, gram = lax.optimization_barrier((gram_of(second, rows), gram))
        qs.append(newton_schulz(*reduce_gram(gram, 4)))
        pair = reduce_gram(gram_second)
        qs.append(newton_schulz(*pair, qs[0]))
    else:
        qs.append(newton_schulz(*reduce_gram(gram)))

    q = qs[-1]
    arrived_q = over_chips(q)
    arrived_rows = [over_chips(total) for total in totals]
    outputs = []
    for distance in range(members):
        if distance:
            q = arrived_q[distance - 1]
            if distance == 1:
                q, *outputs = lax.optimization_barrier((q, *outputs))
        pair_q = over_cores(q)
        for index, size in enumerate(sizes):
            rows_here = totals[index]
            if distance:
                tie = qs[-1] if index == len(sizes) - 1 else pair[0]
                rows_here = lax.optimization_barrier((arrived_rows[index][distance - 1], tie))[0]
            per_block = 2 if size % 2 else 1
            units = size * per_block // CORES
            outputs = apply_side(
                [
                    array.reshape(units, rows // per_block, width)
                    for array in over_cores(rows_here)
                ],
                pair_q,
                params,
                outputs,
                place.reshape(1),
                table,
                CORES * distance,
                qs[index - 1].shape[0] if index else 0,
                size,
                sum(sizes[:index]),
                own,
                padded,
            )
    new_params, update = outputs
    return (new_params, update)


def solution(mesh):
    return jax.shard_map(
        per_device,
        mesh=mesh,
        in_specs=(P("dp", None, "shard", None), P(None, "shard", None), P()),
        out_specs=(P(None, "shard", None), P(None, "shard", None)),
        check_vma=False,
    )
```

```python
import functools
import math

import jax
import jax.numpy as jnp
from jax import lax
from jax.experimental import pallas as pl
from jax.experimental.pallas import tpu as pltpu
from jax.sharding import PartitionSpec as P

D = 7168
V = 128
ITERS = 5
CORES = 2

quintic_one = 3.4445
quintic_two = -4.775
quintic_three = 2.0315
epsilon = 1e-07
learning_rate = 0.02
decay_rate = 0.1
HIGHEST = lax.Precision.HIGHEST


def dot32(left, right):
    return jnp.dot(left, right, precision=HIGHEST, preferred_element_type=jnp.float32)


def newton_kernel(gram_ref, arrived_ref, out_ref):
    items = gram_ref.shape[0]
    rows = lax.broadcasted_iota(jnp.int32, (V, V), 0)
    columns = lax.broadcasted_iota(jnp.int32, (V, V), 1)
    eye = (rows == columns).astype(jnp.float32)
    grams, scales = [], []
    for item in range(items):
        gram = gram_ref[item] + arrived_ref[item]
        norm_value = jnp.sqrt(jnp.sum(gram * eye))
        scale = 1.0 / (norm_value + epsilon)
        scales.append(scale)
        grams.append((gram * scale) * scale)
    products = [None] * items
    for index in range(ITERS):
        squares = [dot32(gram, gram) for gram in grams]
        polys = [
            quintic_one * eye + quintic_two * gram + quintic_three * square
            for gram, square in zip(grams, squares)
        ]
        if index < ITERS - 1:
            halves = [dot32(gram, poly) for gram, poly in zip(grams, polys)]
        if index == 0:
            products = polys
        else:
            products = [dot32(product, poly) for product, poly in zip(products, polys)]
        if index < ITERS - 1:
            grams = [dot32(half, poly) for half, poly in zip(halves, polys)]
    for item in range(items):
        out_ref[item] = products[item] * scales[item]


def newton_schulz(gram, arrived):
    items = gram.shape[0]
    return pl.pallas_call(
        newton_kernel,
        out_shape=jax.ShapeDtypeStruct((items, V, V), jnp.float32),
        in_specs=[pl.BlockSpec(memory_space=pltpu.VMEM)] * 2,
        out_specs=pl.BlockSpec(memory_space=pltpu.VMEM),
        cost_estimate=pl.CostEstimate(
            flops=items * 18 * 12 * V**3, bytes_accessed=items * V * V * 12, transcendentals=0
        ),
        compiler_params=pltpu.CompilerParams(vmem_limit_bytes=16 * 1024 * 1024),
    )(gram, arrived)


def apply_kernel(layout, place_ref, table_ref, *refs):
    count, first, size, offset, own, total, padded = layout
    sources, qs = refs[:count], refs[count : 2 * count]
    params_ref = refs[2 * count]
    new_ref, update_ref, new_buf, update_buf, new_sems, update_sems = refs[-6:]
    per_block = 2 if size % 2 else 1
    units, unit_rows = sources[0].shape[:2]
    whole = size // 2
    place = place_ref[0]

    def locate(source, unit):
        holder = (place ^ source) & (CORES - 1)
        within = holder * units + unit
        block = within >> (per_block - 1)
        index = ((place ^ source) >> (CORES - 1)) * own + offset + block
        head = table_ref[jnp.minimum(index, total - 1) if padded else index]
        start = pl.multiple_of((within & (per_block - 1)) * unit_rows, unit_rows)
        slot = unit
        if per_block > 1:
            slot = jnp.where(block == whole, whole, block - holder * (whole + 1))
        return index < total, head, pl.ds(start, unit_rows), slot

    items = [
        (index, unit, index * units + unit, locate(first + index, unit))
        for index in range(count)
        for unit in range(units)
    ]

    def compute(index, unit, item, head, span, slot):
        q = qs[index][slot]
        high = q.astype(jnp.bfloat16)
        low = (q - high.astype(jnp.float32)).astype(jnp.bfloat16)
        rows = sources[index][unit]
        ortho = jnp.dot(
            jnp.concatenate([rows, rows], axis=1),
            jnp.concatenate([high, low], axis=0),
            preferred_element_type=jnp.float32,
        )
        ortho = ortho.astype(jnp.bfloat16).astype(jnp.float32)
        scaled = 0.2 * math.sqrt(max(D, V)) * ortho
        params = params_ref[head, span]
        new_buf[item] = params - learning_rate * (scaled + decay_rate * params)
        update_buf[item] = scaled.astype(jnp.bfloat16)
        pltpu.make_async_copy(new_buf.at[item], new_ref.at[head, span], new_sems.at[item]).start()
        pltpu.make_async_copy(
            update_buf.at[item], update_ref.at[head, span], update_sems.at[item]
        ).start()

    def finish(item):
        span = pl.ds(0, unit_rows)
        pltpu.make_async_copy(new_buf.at[item], new_ref.at[0, span], new_sems.at[item]).wait()
        pltpu.make_async_copy(
            update_buf.at[item], update_ref.at[0, span], update_sems.at[item]
        ).wait()

    for index, unit, item, (valid, head, span, slot) in items:
        run = functools.partial(compute, index, unit, item, head, span, slot)
        pl.when(valid)(run) if padded else run()
    for index, unit, item, (valid, head, span, slot) in items:
        run = functools.partial(finish, item)
        pl.when(valid)(run) if padded else run()


def apply_side(sources, qs, params, previous, place, table, first, size, offset, own, padded):
    total, rows, width = params.shape
    count = len(sources)
    units, unit_rows = sources[0].shape[:2]
    steps = count * units
    vmem = pl.BlockSpec(memory_space=pltpu.VMEM)
    hbm = pl.BlockSpec(memory_space=pltpu.HBM)
    smem = pl.BlockSpec(memory_space=pltpu.SMEM)
    operands = [place, table, *sources, *qs, params]
    in_specs = [smem, smem] + [vmem] * (2 * count + 1)
    aliases = {}
    for index, array in enumerate(previous):
        aliases[len(operands)] = index
        operands.append(array)
        in_specs.append(hbm)
    work = steps * unit_rows * width
    layout = (count, first, size, offset, own, total, padded)
    return pl.pallas_call(
        functools.partial(apply_kernel, layout),
        in_specs=in_specs,
        out_specs=[hbm, hbm],
        out_shape=[
            jax.ShapeDtypeStruct(params.shape, jnp.float32),
            jax.ShapeDtypeStruct(params.shape, jnp.bfloat16),
        ],
        scratch_shapes=[
            pltpu.VMEM((steps, unit_rows, width), jnp.float32),
            pltpu.VMEM((steps, unit_rows, width), jnp.bfloat16),
            pltpu.SemaphoreType.DMA((steps,)),
            pltpu.SemaphoreType.DMA((steps,)),
        ],
        input_output_aliases=aliases,
        cost_estimate=pl.CostEstimate(flops=4 * work * V, bytes_accessed=12 * work, transcendentals=0),
        compiler_params=pltpu.CompilerParams(vmem_limit_bytes=24 * 1024 * 1024),
    )(*operands)


def chunk_sizes(own):
    if own <= 4:
        return [own]
    return [own - 4, 4]


def swap(array, axis, distance):
    size = lax.axis_size(axis)
    return lax.ppermute(array, axis, [(i, i ^ distance) for i in range(size)])


def gram_of(rows_array, rows):
    blocks = rows_array.reshape(-1, rows, V)
    return jnp.einsum("mrv,mrw->mvw", blocks, blocks, preferred_element_type=jnp.float32)


def per_device(grads, params, table):
    local = grads[0]
    count, rows, width = local.shape
    replicas = lax.axis_size("dp")
    groups = lax.axis_size("shard")
    members = replicas // CORES
    own = -(-count // members)
    padded = members * own > count
    place = lax.axis_index("dp").astype(jnp.int32)
    core = place % CORES
    member = place // CORES
    if padded:
        filler = jnp.zeros((members * own - count, rows, width), local.dtype)
        local = jnp.concatenate([local, filler], axis=0)
    flat = local.reshape(members * own * rows, width)
    sizes = chunk_sizes(own)

    def rows_of(chip, offset, which, length):
        return lax.dynamic_slice_in_dim(flat, (chip * own + offset) * rows + which * length, length)

    def total_of(terms):
        terms = [term.astype(jnp.float32) for term in terms]
        while len(terms) > 1:
            terms = [sum(terms[i : i + 2][1:], terms[i]) for i in range(0, len(terms), 2)]
        return terms[0]

    def reduce_gram(gram, distance=1):
        while True:
            arrived = swap(gram, "shard", distance)
            distance *= 2
            if distance >= groups:
                return gram, arrived
            gram = gram + arrived

    def over_chips(array):
        return [swap(array, "dp", distance * CORES) for distance in range(1, members)]

    def over_cores(array):
        return [array, swap(array, "dp", 1)]

    def pieces_of(offset, size):
        share = size * rows // CORES
        return [
            rows_of((place ^ distance) // CORES, offset, (place ^ distance) % CORES, share)
            for distance in range(replicas)
        ]

    def exchange(pieces):
        return [swap(piece, "dp", d) if d else piece for d, piece in enumerate(pieces)]

    size = sizes[0]
    terms = exchange(pieces_of(0, size))
    if len(sizes) > 1:
        offset, length = size, sizes[1] * rows
        share = length // CORES
        chunks = [rows_of(member ^ d, offset, 0, length) for d in range(members)]
        to_core = rows_of(member, offset, 1 - core, share)
        terms[-1], to_core, *chunks = lax.optimization_barrier((terms[-1], to_core, *chunks))
        chunks = [swap(chunk, "dp", d * CORES) if d else chunk for d, chunk in enumerate(chunks)]
        seconds = [rows_of(member, offset, core, share), swap(to_core, "dp", 1)]

    first = total_of(terms).astype(jnp.bfloat16)
    whole = size // 2
    if size % 2:
        half = lax.dynamic_slice_in_dim(first, (1 - core) * whole * rows, rows // 2)
        gram = gram_of(half, rows // 2)
        gram = gram + swap(gram, "dp", 1)
        if whole:
            full = lax.dynamic_slice_in_dim(first, core * (rows // 2), whole * rows)
            gram = jnp.concatenate([gram_of(full, rows), gram], axis=0)
    else:
        gram = gram_of(first, rows)
    totals, qs = [first], []
    first_arrived = over_chips(first)
    if len(sizes) > 1:
        gram = gram + swap(gram, "shard", 1)
        gram = gram + swap(gram, "shard", 2)
        *arrived, gram = lax.optimization_barrier((*chunks[1:], gram))
        for chunk in arrived:
            seconds.append(lax.dynamic_slice_in_dim(chunk, core * share, share))
            passed = lax.dynamic_slice_in_dim(chunk, (1 - core) * share, share)
            seconds.append(swap(passed, "dp", 1))
        second = total_of(seconds).astype(jnp.bfloat16)
        totals.append(second)
        gram, arrived = reduce_gram(gram, 4)
        gram_second = gram_of(second, rows)
        gram_second = gram_second + swap(gram_second, "shard", 1)
        arrived, gram_second = lax.optimization_barrier((arrived, gram_second))
        qs.append(newton_schulz(gram, arrived))
        gram_second = gram_second + swap(gram_second, "shard", 2)
        *first_arrived, gram_second = lax.optimization_barrier((*first_arrived, gram_second))
        qs.append(newton_schulz(*reduce_gram(gram_second, 4)))
    else:
        qs.append(newton_schulz(*reduce_gram(gram)))

    arrived_q = [over_chips(q) for q in qs]
    arrived_rows = [first_arrived, *(over_chips(total) for total in totals[1:])]
    outputs = []
    for distance in range(members):
        rows_here, q_here = totals, qs
        if distance:
            rows_here = [arrived[distance - 1] for arrived in arrived_rows]
            q_here = [arrived[distance - 1] for arrived in arrived_q]
        if distance == 1:
            rest = (rows_here[-1], *q_here, *outputs)
            rows_here[-1], *rest = lax.optimization_barrier(rest)
            q_here, outputs = rest[: len(qs)], rest[len(qs) :]
        for index, size in enumerate(sizes):
            per_block = 2 if size % 2 else 1
            units = size * per_block // CORES
            outputs = apply_side(
                [
                    array.reshape(units, rows // per_block, width)
                    for array in over_cores(rows_here[index])
                ],
                over_cores(q_here[index]),
                params,
                outputs,
                place.reshape(1),
                table,
                CORES * distance,
                size,
                sum(sizes[:index]),
                own,
                padded,
            )
    new_params, update = outputs
    return (new_params, update)


def solution(mesh):
    return jax.shard_map(
        per_device,
        mesh=mesh,
        in_specs=(P("dp", None, "shard", None), P(None, "shard", None), P()),
        out_specs=(P(None, "shard", None), P(None, "shard", None)),
        check_vma=False,
    )
```

```python
import functools
import math

import jax
import jax.numpy as jnp
from jax import lax
from jax.experimental import pallas as pl
from jax.experimental.pallas import tpu as pltpu
from jax.sharding import PartitionSpec as P

D = 7168
V = 128
ITERS = 5
CORES = 2

quintic_one = 3.4445
quintic_two = -4.775
quintic_three = 2.0315
epsilon = 1e-07
learning_rate = 0.02
decay_rate = 0.1
HIGHEST = lax.Precision.HIGHEST


def dot32(left, right):
    return jnp.dot(left, right, precision=HIGHEST, preferred_element_type=jnp.float32)


def newton_kernel(gram_ref, arrived_ref, *refs):
    *earlier, out_ref = refs
    skip = 0
    for ref in earlier:
        out_ref[: ref.shape[0]] = ref[...]
        skip = ref.shape[0]
    items = gram_ref.shape[0]
    rows = lax.broadcasted_iota(jnp.int32, (V, V), 0)
    columns = lax.broadcasted_iota(jnp.int32, (V, V), 1)
    eye = (rows == columns).astype(jnp.float32)
    grams, scales = [], []
    for item in range(items):
        gram = gram_ref[item] + arrived_ref[item]
        norm_value = jnp.sqrt(jnp.sum(gram * eye))
        scale = 1.0 / (norm_value + epsilon)
        scales.append(scale)
        grams.append((gram * scale) * scale)
    products = [None] * items
    for index in range(ITERS):
        squares = [dot32(gram, gram) for gram in grams]
        polys = [
            quintic_one * eye + quintic_two * gram + quintic_three * square
            for gram, square in zip(grams, squares)
        ]
        if index < ITERS - 1:
            halves = [dot32(gram, poly) for gram, poly in zip(grams, polys)]
        if index == 0:
            products = polys
        else:
            products = [dot32(product, poly) for product, poly in zip(products, polys)]
        if index < ITERS - 1:
            grams = [dot32(half, poly) for half, poly in zip(halves, polys)]
    for item in range(items):
        out_ref[skip + item] = products[item] * scales[item]


def newton_schulz(gram, arrived, *earlier):
    items = gram.shape[0]
    slots = items + sum(q.shape[0] for q in earlier)
    return pl.pallas_call(
        newton_kernel,
        out_shape=jax.ShapeDtypeStruct((slots, V, V), jnp.float32),
        in_specs=[pl.BlockSpec(memory_space=pltpu.VMEM)] * (2 + len(earlier)),
        out_specs=pl.BlockSpec(memory_space=pltpu.VMEM),
        cost_estimate=pl.CostEstimate(
            flops=items * 18 * 12 * V**3, bytes_accessed=items * V * V * 12, transcendentals=0
        ),
        compiler_params=pltpu.CompilerParams(vmem_limit_bytes=16 * 1024 * 1024),
    )(gram, arrived, *earlier)


def apply_kernel(layout, place_ref, table_ref, *refs):
    count, first, base, size, offset, own, total, padded = layout
    sources, qs = refs[:count], refs[count : 2 * count]
    params_ref = refs[2 * count]
    new_ref, update_ref, new_buf, update_buf, new_sems, update_sems = refs[-6:]
    per_block = 2 if size % 2 else 1
    units, unit_rows = sources[0].shape[:2]
    whole = size // 2
    place = place_ref[0]

    def locate(source, unit):
        holder = (place ^ source) & (CORES - 1)
        within = holder * units + unit
        block = within >> (per_block - 1)
        index = ((place ^ source) >> (CORES - 1)) * own + offset + block
        head = table_ref[jnp.minimum(index, total - 1) if padded else index]
        start = pl.multiple_of((within & (per_block - 1)) * unit_rows, unit_rows)
        slot = unit
        if per_block > 1:
            slot = jnp.where(block == whole, whole, block - holder * (whole + 1))
        return index < total, head, pl.ds(start, unit_rows), base + slot

    items = [
        (index, unit, index * units + unit, locate(first + index, unit))
        for index in range(count)
        for unit in range(units)
    ]

    def compute(index, unit, item, head, span, slot):
        q = qs[index][slot]
        high = q.astype(jnp.bfloat16)
        low = (q - high.astype(jnp.float32)).astype(jnp.bfloat16)
        rows = sources[index][unit]
        ortho = jnp.dot(
            jnp.concatenate([rows, rows], axis=1),
            jnp.concatenate([high, low], axis=0),
            preferred_element_type=jnp.float32,
        )
        ortho = ortho.astype(jnp.bfloat16).astype(jnp.float32)
        scaled = 0.2 * math.sqrt(max(D, V)) * ortho
        params = params_ref[head, span]
        new_buf[item] = params - learning_rate * (scaled + decay_rate * params)
        update_buf[item] = scaled.astype(jnp.bfloat16)
        pltpu.make_async_copy(new_buf.at[item], new_ref.at[head, span], new_sems.at[item]).start()
        pltpu.make_async_copy(
            update_buf.at[item], update_ref.at[head, span], update_sems.at[item]
        ).start()

    def finish(item):
        span = pl.ds(0, unit_rows)
        pltpu.make_async_copy(new_buf.at[item], new_ref.at[0, span], new_sems.at[item]).wait()
        pltpu.make_async_copy(
            update_buf.at[item], update_ref.at[0, span], update_sems.at[item]
        ).wait()

    for index, unit, item, (valid, head, span, slot) in items:
        run = functools.partial(compute, index, unit, item, head, span, slot)
        pl.when(valid)(run) if padded else run()
    for index, unit, item, (valid, head, span, slot) in items:
        run = functools.partial(finish, item)
        pl.when(valid)(run) if padded else run()


def apply_side(sources, qs, params, previous, place, table, first, base, size, offset, own, padded):
    total, rows, width = params.shape
    count = len(sources)
    units, unit_rows = sources[0].shape[:2]
    steps = count * units
    vmem = pl.BlockSpec(memory_space=pltpu.VMEM)
    hbm = pl.BlockSpec(memory_space=pltpu.HBM)
    smem = pl.BlockSpec(memory_space=pltpu.SMEM)
    operands = [place, table, *sources, *qs, params]
    in_specs = [smem, smem] + [vmem] * (2 * count + 1)
    aliases = {}
    for index, array in enumerate(previous):
        aliases[len(operands)] = index
        operands.append(array)
        in_specs.append(hbm)
    work = steps * unit_rows * width
    layout = (count, first, base, size, offset, own, total, padded)
    return pl.pallas_call(
        functools.partial(apply_kernel, layout),
        in_specs=in_specs,
        out_specs=[hbm, hbm],
        out_shape=[
            jax.ShapeDtypeStruct(params.shape, jnp.float32),
            jax.ShapeDtypeStruct(params.shape, jnp.bfloat16),
        ],
        scratch_shapes=[
            pltpu.VMEM((steps, unit_rows, width), jnp.float32),
            pltpu.VMEM((steps, unit_rows, width), jnp.bfloat16),
            pltpu.SemaphoreType.DMA((steps,)),
            pltpu.SemaphoreType.DMA((steps,)),
        ],
        input_output_aliases=aliases,
        cost_estimate=pl.CostEstimate(flops=4 * work * V, bytes_accessed=12 * work, transcendentals=0),
        compiler_params=pltpu.CompilerParams(vmem_limit_bytes=24 * 1024 * 1024),
    )(*operands)


def chunk_sizes(own):
    if own <= 4:
        return [own]
    return [own - 4, 4]


def swap(array, axis, distance):
    size = lax.axis_size(axis)
    return lax.ppermute(array, axis, [(i, i ^ distance) for i in range(size)])


def gram_of(rows_array, rows):
    blocks = rows_array.reshape(-1, rows, V)
    return jnp.einsum("mrv,mrw->mvw", blocks, blocks, preferred_element_type=jnp.float32)


def per_device(grads, params, table):
    local = grads[0]
    count, rows, width = local.shape
    replicas = lax.axis_size("dp")
    groups = lax.axis_size("shard")
    members = replicas // CORES
    own = -(-count // members)
    padded = members * own > count
    place = lax.axis_index("dp").astype(jnp.int32)
    core = place % CORES
    member = place // CORES
    if padded:
        filler = jnp.zeros((members * own - count, rows, width), local.dtype)
        local = jnp.concatenate([local, filler], axis=0)
    flat = local.reshape(members * own * rows, width)
    sizes = chunk_sizes(own)

    def rows_of(chip, offset, which, length):
        return lax.dynamic_slice_in_dim(flat, (chip * own + offset) * rows + which * length, length)

    def total_of(terms):
        terms = [term.astype(jnp.float32) for term in terms]
        while len(terms) > 1:
            terms = [sum(terms[i : i + 2][1:], terms[i]) for i in range(0, len(terms), 2)]
        return terms[0]

    def reduce_gram(gram, distance=1):
        while True:
            arrived = swap(gram, "shard", distance)
            distance *= 2
            if distance >= groups:
                return gram, arrived
            gram = gram + arrived

    def over_chips(array):
        return [swap(array, "dp", distance * CORES) for distance in range(1, members)]

    def over_cores(array):
        return [array, swap(array, "dp", 1)]

    def pieces_of(offset, size):
        share = size * rows // CORES
        return [
            rows_of((place ^ distance) // CORES, offset, (place ^ distance) % CORES, share)
            for distance in range(replicas)
        ]

    def exchange(pieces):
        return [swap(piece, "dp", d) if d else piece for d, piece in enumerate(pieces)]

    size = sizes[0]
    terms = exchange(pieces_of(0, size))
    seconds = []
    if len(sizes) > 1:
        pieces = pieces_of(size, sizes[1])
        terms[-1], *pieces = lax.optimization_barrier((terms[-1], *pieces))
        *seconds, late = exchange(pieces)

    first = total_of(terms).astype(jnp.bfloat16)
    whole = size // 2
    if size % 2:
        half = lax.dynamic_slice_in_dim(first, (1 - core) * whole * rows, rows // 2)
        gram = gram_of(half, rows // 2)
        gram = gram + swap(gram, "dp", 1)
        if whole:
            full = lax.dynamic_slice_in_dim(first, core * (rows // 2), whole * rows)
            gram = jnp.concatenate([gram_of(full, rows), gram], axis=0)
    else:
        gram = gram_of(first, rows)
    totals, qs = [first], []
    if seconds:
        *seconds, gram = lax.optimization_barrier((*seconds, gram))
        gram = gram + swap(gram, "shard", 1)
        late, gram = lax.optimization_barrier((late, gram))
        gram = gram + swap(gram, "shard", 2)
        second = total_of([*seconds, late]).astype(jnp.bfloat16)
        totals.append(second)
        gram_second, gram = lax.optimization_barrier((gram_of(second, rows), gram))
        qs.append(newton_schulz(*reduce_gram(gram, 4)))
        pair = reduce_gram(gram_second)
        qs.append(newton_schulz(*pair, qs[0]))
    else:
        qs.append(newton_schulz(*reduce_gram(gram)))

    q = qs[-1]
    arrived_q = over_chips(q)
    arrived_rows = [over_chips(total) for total in totals]
    outputs = []
    for distance in range(members):
        if distance:
            q = arrived_q[distance - 1]
            if distance == 1:
                q, *outputs = lax.optimization_barrier((q, *outputs))
        pair_q = over_cores(q)
        for index, size in enumerate(sizes):
            rows_here = totals[index]
            if distance:
                tie = qs[-1] if index == len(sizes) - 1 else pair[0]
                rows_here = lax.optimization_barrier((arrived_rows[index][distance - 1], tie))[0]
            per_block = 2 if size % 2 else 1
            units = size * per_block // CORES
            outputs = apply_side(
                [
                    array.reshape(units, rows // per_block, width)
                    for array in over_cores(rows_here)
                ],
                pair_q,
                params,
                outputs,
                place.reshape(1),
                table,
                CORES * distance,
                qs[index - 1].shape[0] if index else 0,
                size,
                sum(sizes[:index]),
                own,
                padded,
            )
    new_params, update = outputs
    return (new_params, update)


def solution(mesh):
    return jax.shard_map(
        per_device,
        mesh=mesh,
        in_specs=(P("dp", None, "shard", None), P(None, "shard", None), P()),
        out_specs=(P(None, "shard", None), P(None, "shard", None)),
        check_vma=False,
    )
```

```python
import functools
import math

import jax
import jax.numpy as jnp
from jax import lax
from jax.experimental import pallas as pl
from jax.experimental.pallas import tpu as pltpu
from jax.sharding import PartitionSpec as P

D = 7168
V = 128
ITERS = 5
CORES = 2

quintic_one = 3.4445
quintic_two = -4.775
quintic_three = 2.0315
epsilon = 1e-07
learning_rate = 0.02
decay_rate = 0.1
HIGHEST = lax.Precision.HIGHEST


def dot32(left, right):
    return jnp.dot(left, right, precision=HIGHEST, preferred_element_type=jnp.float32)


def newton_kernel(gram_ref, arrived_ref, *refs):
    *earlier, out_ref = refs
    skip = 0
    for ref in earlier:
        out_ref[: ref.shape[0]] = ref[...]
        skip = ref.shape[0]
    items = gram_ref.shape[0]
    rows = lax.broadcasted_iota(jnp.int32, (V, V), 0)
    columns = lax.broadcasted_iota(jnp.int32, (V, V), 1)
    eye = (rows == columns).astype(jnp.float32)
    grams, scales = [], []
    for item in range(items):
        gram = gram_ref[item] + arrived_ref[item]
        norm_value = jnp.sqrt(jnp.sum(gram * eye))
        scale = 1.0 / (norm_value + epsilon)
        scales.append(scale)
        grams.append((gram * scale) * scale)
    products = [None] * items
    for index in range(ITERS):
        squares = [dot32(gram, gram) for gram in grams]
        polys = [
            quintic_one * eye + quintic_two * gram + quintic_three * square
            for gram, square in zip(grams, squares)
        ]
        if index < ITERS - 1:
            halves = [dot32(gram, poly) for gram, poly in zip(grams, polys)]
        if index == 0:
            products = polys
        else:
            products = [dot32(product, poly) for product, poly in zip(products, polys)]
        if index < ITERS - 1:
            grams = [dot32(half, poly) for half, poly in zip(halves, polys)]
    for item in range(items):
        out_ref[skip + item] = products[item] * scales[item]


def newton_schulz(gram, arrived, *earlier):
    items = gram.shape[0]
    slots = items + sum(q.shape[0] for q in earlier)
    return pl.pallas_call(
        newton_kernel,
        out_shape=jax.ShapeDtypeStruct((slots, V, V), jnp.float32),
        in_specs=[pl.BlockSpec(memory_space=pltpu.VMEM)] * (2 + len(earlier)),
        out_specs=pl.BlockSpec(memory_space=pltpu.VMEM),
        cost_estimate=pl.CostEstimate(
            flops=items * 18 * 12 * V**3, bytes_accessed=items * V * V * 12, transcendentals=0
        ),
        compiler_params=pltpu.CompilerParams(vmem_limit_bytes=16 * 1024 * 1024),
    )(gram, arrived, *earlier)


def apply_kernel(layout, place_ref, table_ref, *refs):
    count, kinds, first, bases, size, offset, own, total, padded = layout
    sources, refs = refs[:count], refs[count:]
    new_ref, update_ref, new_buf, update_buf, q_buf, new_sems, update_sems = refs[-7:]
    qs, params_ref = refs[: kinds * count], refs[kinds * count]
    per_block = 2 if size % 2 else 1
    units, unit_rows = sources[0].shape[:2]
    whole = size // 2
    kept_base, other_base, half = bases
    place, side = place_ref[0], place_ref[1]
    for index in range(count):
        skip = 0
        for q_ref in qs[index * kinds : (index + 1) * kinds]:
            q_buf[index, pl.ds(skip, q_ref.shape[0])] = q_ref[...]
            skip += q_ref.shape[0]

    def locate(source, unit):
        holder = (place ^ source) & (CORES - 1)
        within = holder * units + unit
        block = within >> (per_block - 1)
        index = ((place ^ source) >> (CORES - 1)) * own + offset + block
        head = table_ref[jnp.minimum(index, total - 1) if padded else index]
        start = pl.multiple_of((within & (per_block - 1)) * unit_rows, unit_rows)
        number = block - holder * (size - whole)
        slot = kept_base + number
        if half:
            mine = (number >= side * half) & (number < (side + 1) * half)
            slot = jnp.where(
                mine, slot - side * half, other_base + number - (1 - side) * half
            )
        if size % 2:
            slot = jnp.where(block == whole, kept_base - 1, slot)
        return index < total, head, pl.ds(start, unit_rows), slot

    items = [
        (index, unit, index * units + unit, locate(first + index, unit))
        for index in range(count)
        for unit in range(units)
    ]

    def compute(index, unit, item, head, span, slot):
        q = q_buf[index, slot]
        high = q.astype(jnp.bfloat16)
        low = (q - high.astype(jnp.float32)).astype(jnp.bfloat16)
        rows = sources[index][unit]
        ortho = jnp.dot(
            jnp.concatenate([rows, rows], axis=1),
            jnp.concatenate([high, low], axis=0),
            preferred_element_type=jnp.float32,
        )
        ortho = ortho.astype(jnp.bfloat16).astype(jnp.float32)
        scaled = 0.2 * math.sqrt(max(D, V)) * ortho
        params = params_ref[head, span]
        new_buf[item] = params - learning_rate * (scaled + decay_rate * params)
        update_buf[item] = scaled.astype(jnp.bfloat16)
        pltpu.make_async_copy(new_buf.at[item], new_ref.at[head, span], new_sems.at[item]).start()
        pltpu.make_async_copy(
            update_buf.at[item], update_ref.at[head, span], update_sems.at[item]
        ).start()

    def finish(item):
        span = pl.ds(0, unit_rows)
        pltpu.make_async_copy(new_buf.at[item], new_ref.at[0, span], new_sems.at[item]).wait()
        pltpu.make_async_copy(
            update_buf.at[item], update_ref.at[0, span], update_sems.at[item]
        ).wait()

    for index, unit, item, (valid, head, span, slot) in items:
        run = functools.partial(compute, index, unit, item, head, span, slot)
        pl.when(valid)(run) if padded else run()
    for index, unit, item, (valid, head, span, slot) in items:
        run = functools.partial(finish, item)
        pl.when(valid)(run) if padded else run()


def apply_side(sources, qs, params, previous, place, table, first, bases, size, offset, own, padded):
    total, rows, width = params.shape
    count = len(sources)
    units, unit_rows = sources[0].shape[:2]
    steps = count * units
    vmem = pl.BlockSpec(memory_space=pltpu.VMEM)
    hbm = pl.BlockSpec(memory_space=pltpu.HBM)
    smem = pl.BlockSpec(memory_space=pltpu.SMEM)
    operands = [place, table, *sources, *qs, params]
    in_specs = [smem, smem] + [vmem] * (count + len(qs) + 1)
    aliases = {}
    for index, array in enumerate(previous):
        aliases[len(operands)] = index
        operands.append(array)
        in_specs.append(hbm)
    work = steps * unit_rows * width
    layout = (count, len(qs) // count, first, bases, size, offset, own, total, padded)
    return pl.pallas_call(
        functools.partial(apply_kernel, layout),
        in_specs=in_specs,
        out_specs=[hbm, hbm],
        out_shape=[
            jax.ShapeDtypeStruct(params.shape, jnp.float32),
            jax.ShapeDtypeStruct(params.shape, jnp.bfloat16),
        ],
        scratch_shapes=[
            pltpu.VMEM((steps, unit_rows, width), jnp.float32),
            pltpu.VMEM((steps, unit_rows, width), jnp.bfloat16),
            pltpu.VMEM((count, sum(q.shape[0] for q in qs) // count, V, V), jnp.float32),
            pltpu.SemaphoreType.DMA((steps,)),
            pltpu.SemaphoreType.DMA((steps,)),
        ],
        input_output_aliases=aliases,
        cost_estimate=pl.CostEstimate(flops=4 * work * V, bytes_accessed=12 * work, transcendentals=0),
        compiler_params=pltpu.CompilerParams(vmem_limit_bytes=24 * 1024 * 1024),
    )(*operands)


def chunk_sizes(own):
    if own <= 4:
        return [own]
    return [own - 4, 4]


def swap(array, axis, distance):
    size = lax.axis_size(axis)
    return lax.ppermute(array, axis, [(i, i ^ distance) for i in range(size)])


def gram_of(rows_array, rows):
    blocks = rows_array.reshape(-1, rows, V)
    return jnp.einsum("mrv,mrw->mvw", blocks, blocks, preferred_element_type=jnp.float32)


def per_device(grads, params, table):
    local = grads[0]
    count, rows, width = local.shape
    replicas = lax.axis_size("dp")
    groups = lax.axis_size("shard")
    members = replicas // CORES
    own = -(-count // members)
    padded = members * own > count
    place = lax.axis_index("dp").astype(jnp.int32)
    core = place % CORES
    member = place // CORES
    side = lax.axis_index("shard").astype(jnp.int32) % 2
    if padded:
        filler = jnp.zeros((members * own - count, rows, width), local.dtype)
        local = jnp.concatenate([local, filler], axis=0)
    flat = local.reshape(members * own * rows, width)
    sizes = chunk_sizes(own)

    def rows_of(chip, offset, which, length):
        return lax.dynamic_slice_in_dim(flat, (chip * own + offset) * rows + which * length, length)

    def total_of(terms):
        terms = [term.astype(jnp.float32) for term in terms]
        while len(terms) > 1:
            terms = [sum(terms[i : i + 2][1:], terms[i]) for i in range(0, len(terms), 2)]
        return terms[0]

    def reduce_gram(gram, distance):
        while True:
            arrived = swap(gram, "shard", distance)
            distance *= 2
            if distance >= groups:
                return gram, arrived
            gram = gram + arrived

    def first_stage(middle, whole):
        count_whole = whole.shape[0]
        if count_whole == 0 or count_whole % 2:
            gram = jnp.concatenate([*middle, whole], axis=0)
            return gram + swap(gram, "shard", 1)
        half = count_whole // 2
        keep = lax.dynamic_slice_in_dim(whole, side * half, half)
        send = lax.dynamic_slice_in_dim(whole, (1 - side) * half, half)
        if middle:
            keep = jnp.concatenate([*middle, keep], axis=0)
            send = jnp.concatenate([*middle, send], axis=0)
        return keep + swap(send, "shard", 1)

    def over_chips(array):
        return [swap(array, "dp", distance * CORES) for distance in range(1, members)]

    def over_cores(array):
        return [array, swap(array, "dp", 1)]

    def pieces_of(offset, size):
        share = size * rows // CORES
        return [
            rows_of((place ^ distance) // CORES, offset, (place ^ distance) % CORES, share)
            for distance in range(replicas)
        ]

    def exchange(pieces):
        return [swap(piece, "dp", d) if d else piece for d, piece in enumerate(pieces)]

    size = sizes[0]
    terms = exchange(pieces_of(0, size))
    seconds = []
    if len(sizes) > 1:
        pieces = pieces_of(size, sizes[1])
        terms[-1], *pieces = lax.optimization_barrier((terms[-1], *pieces))
        *seconds, late = exchange(pieces)

    first = total_of(terms).astype(jnp.bfloat16)
    whole = size // 2
    middle = []
    full = first
    if size % 2:
        half = lax.dynamic_slice_in_dim(first, (1 - core) * whole * rows, rows // 2)
        gram = gram_of(half, rows // 2)
        middle = [gram + swap(gram, "dp", 1)]
        full = lax.dynamic_slice_in_dim(first, core * (rows // 2), whole * rows)
    grams = gram_of(full, rows) if whole else jnp.zeros((0, V, V), jnp.float32)
    totals, qs = [first], []
    if seconds:
        *seconds, grams, middle = lax.optimization_barrier((*seconds, grams, middle))
        gram = first_stage(middle, grams)
        late, gram = lax.optimization_barrier((late, gram))
        gram = gram + swap(gram, "shard", 2)
        second = total_of([*seconds, late]).astype(jnp.bfloat16)
        totals.append(second)
        gram_second, gram = lax.optimization_barrier((gram_of(second, rows), gram))
        qs.append(newton_schulz(*reduce_gram(gram, 4)))
        pair = reduce_gram(first_stage([], gram_second), 2)
        qs.append(newton_schulz(*pair, qs[0]))
    else:
        qs.append(newton_schulz(*reduce_gram(first_stage(middle, grams), 2)))

    halves = [0 if (size // 2) % 2 else size // 4 for size in sizes]
    odd = sizes[0] % 2
    kept_bases, other_bases = [odd], [qs[-1].shape[0]]
    for size, half in zip(sizes, halves):
        kept_bases.append(kept_bases[-1] + (half or size // 2))
        other_bases.append(other_bases[-1] + half)
    shared = kept_bases[0] if halves[0] else kept_bases[1]

    def both_sides(q):
        if not any(halves):
            return [q]
        return [q, swap(q[shared:], "shard", 1)]

    scalars = jnp.stack([place, side])
    q = qs[-1]
    arrived_q = over_chips(q)
    arrived_rows = [over_chips(total) for total in totals]
    outputs = []
    waiting = None
    for distance in range(members):
        if distance:
            q = waiting if waiting is not None else arrived_q[distance - 1]
            waiting = None
        kinds = [over_cores(array) for array in both_sides(q)]
        pair_q = [kind[which] for which in range(CORES) for kind in kinds]
        for index, size in enumerate(sizes):
            rows_here = totals[index]
            if distance:
                tie = qs[-1] if index == len(sizes) - 1 else pair[0]
                rows_here = lax.optimization_barrier((arrived_rows[index][distance - 1], tie))[0]
            per_block = 2 if size % 2 else 1
            units = size * per_block // CORES
            outputs = apply_side(
                [
                    array.reshape(units, rows // per_block, width)
                    for array in over_cores(rows_here)
                ],
                pair_q,
                params,
                outputs,
                scalars,
                table,
                CORES * distance,
                (kept_bases[index], other_bases[index], halves[index]),
                size,
                sum(sizes[:index]),
                own,
                padded,
            )
            if distance == 0 and index == 0:
                waiting, *outputs = lax.optimization_barrier((arrived_q[0], *outputs))
    new_params, update = outputs
    return (new_params, update)


def solution(mesh):
    return jax.shard_map(
        per_device,
        mesh=mesh,
        in_specs=(P("dp", None, "shard", None), P(None, "shard", None), P()),
        out_specs=(P(None, "shard", None), P(None, "shard", None)),
        check_vma=False,
    )
```

```python
import functools
import math

import jax
import jax.numpy as jnp
from jax import lax
from jax.experimental import pallas as pl
from jax.experimental.pallas import tpu as pltpu
from jax.sharding import PartitionSpec as P

D = 7168
V = 128
ITERS = 5
CORES = 2

quintic_one = 3.4445
quintic_two = -4.775
quintic_three = 2.0315
epsilon = 1e-07
learning_rate = 0.02
decay_rate = 0.1
HIGHEST = lax.Precision.HIGHEST


def dot32(left, right):
    return jnp.dot(left, right, precision=HIGHEST, preferred_element_type=jnp.float32)


def newton_kernel(gram_ref, arrived_ref, *refs):
    *earlier, out_ref = refs
    skip = 0
    for ref in earlier:
        out_ref[: ref.shape[0]] = ref[...]
        skip = ref.shape[0]
    items = gram_ref.shape[0]
    rows = lax.broadcasted_iota(jnp.int32, (V, V), 0)
    columns = lax.broadcasted_iota(jnp.int32, (V, V), 1)
    eye = (rows == columns).astype(jnp.float32)
    grams, scales = [], []
    for item in range(items):
        gram = gram_ref[item] + arrived_ref[item]
        norm_value = jnp.sqrt(jnp.sum(gram * eye))
        scale = 1.0 / (norm_value + epsilon)
        scales.append(scale)
        grams.append((gram * scale) * scale)
    products = [None] * items
    for index in range(ITERS):
        squares = [dot32(gram, gram) for gram in grams]
        polys = [
            quintic_one * eye + quintic_two * gram + quintic_three * square
            for gram, square in zip(grams, squares)
        ]
        if index < ITERS - 1:
            halves = [dot32(gram, poly) for gram, poly in zip(grams, polys)]
        if index == 0:
            products = polys
        else:
            products = [dot32(product, poly) for product, poly in zip(products, polys)]
        if index < ITERS - 1:
            grams = [dot32(half, poly) for half, poly in zip(halves, polys)]
    for item in range(items):
        out_ref[skip + item] = products[item] * scales[item]


def newton_schulz(gram, arrived, *earlier):
    items = gram.shape[0]
    slots = items + sum(q.shape[0] for q in earlier)
    return pl.pallas_call(
        newton_kernel,
        out_shape=jax.ShapeDtypeStruct((slots, V, V), jnp.float32),
        in_specs=[pl.BlockSpec(memory_space=pltpu.VMEM)] * (2 + len(earlier)),
        out_specs=pl.BlockSpec(memory_space=pltpu.VMEM),
        cost_estimate=pl.CostEstimate(
            flops=items * 18 * 12 * V**3, bytes_accessed=items * V * V * 12, transcendentals=0
        ),
        compiler_params=pltpu.CompilerParams(vmem_limit_bytes=16 * 1024 * 1024),
    )(gram, arrived, *earlier)


def apply_kernel(layout, place_ref, table_ref, *refs):
    count, first, base, size, offset, own, total, padded = layout
    sources, qs = refs[:count], refs[count : 2 * count]
    params_ref = refs[2 * count]
    new_ref, update_ref, new_buf, update_buf, new_sems, update_sems = refs[-6:]
    per_block = 2 if size % 2 else 1
    units, unit_rows = sources[0].shape[:2]
    whole = size // 2
    place = place_ref[0]

    def locate(source, unit):
        holder = (place ^ source) & (CORES - 1)
        within = holder * units + unit
        block = within >> (per_block - 1)
        index = ((place ^ source) >> (CORES - 1)) * own + offset + block
        head = table_ref[jnp.minimum(index, total - 1) if padded else index]
        start = pl.multiple_of((within & (per_block - 1)) * unit_rows, unit_rows)
        slot = unit
        if per_block > 1:
            slot = jnp.where(block == whole, whole, block - holder * (whole + 1))
        return index < total, head, pl.ds(start, unit_rows), base + slot

    items = [
        (index, unit, index * units + unit, locate(first + index, unit))
        for index in range(count)
        for unit in range(units)
    ]

    def compute(index, unit, item, head, span, slot):
        q = qs[index][slot]
        high = q.astype(jnp.bfloat16)
        low = (q - high.astype(jnp.float32)).astype(jnp.bfloat16)
        rows = sources[index][unit]
        ortho = jnp.dot(
            jnp.concatenate([rows, rows], axis=1),
            jnp.concatenate([high, low], axis=0),
            preferred_element_type=jnp.float32,
        )
        ortho = ortho.astype(jnp.bfloat16).astype(jnp.float32)
        scaled = 0.2 * math.sqrt(max(D, V)) * ortho
        params = params_ref[head, span]
        new_buf[item] = params - learning_rate * (scaled + decay_rate * params)
        update_buf[item] = scaled.astype(jnp.bfloat16)
        pltpu.make_async_copy(new_buf.at[item], new_ref.at[head, span], new_sems.at[item]).start()
        pltpu.make_async_copy(
            update_buf.at[item], update_ref.at[head, span], update_sems.at[item]
        ).start()

    def finish(item):
        span = pl.ds(0, unit_rows)
        pltpu.make_async_copy(new_buf.at[item], new_ref.at[0, span], new_sems.at[item]).wait()
        pltpu.make_async_copy(
            update_buf.at[item], update_ref.at[0, span], update_sems.at[item]
        ).wait()

    for index, unit, item, (valid, head, span, slot) in items:
        run = functools.partial(compute, index, unit, item, head, span, slot)
        pl.when(valid)(run) if padded else run()
    for index, unit, item, (valid, head, span, slot) in items:
        run = functools.partial(finish, item)
        pl.when(valid)(run) if padded else run()


def apply_side(sources, qs, params, previous, place, table, first, base, size, offset, own, padded):
    total, rows, width = params.shape
    count = len(sources)
    units, unit_rows = sources[0].shape[:2]
    steps = count * units
    vmem = pl.BlockSpec(memory_space=pltpu.VMEM)
    hbm = pl.BlockSpec(memory_space=pltpu.HBM)
    smem = pl.BlockSpec(memory_space=pltpu.SMEM)
    operands = [place, table, *sources, *qs, params]
    in_specs = [smem, smem] + [vmem] * (2 * count + 1)
    aliases = {}
    for index, array in enumerate(previous):
        aliases[len(operands)] = index
        operands.append(array)
        in_specs.append(hbm)
    work = steps * unit_rows * width
    layout = (count, first, base, size, offset, own, total, padded)
    return pl.pallas_call(
        functools.partial(apply_kernel, layout),
        in_specs=in_specs,
        out_specs=[hbm, hbm],
        out_shape=[
            jax.ShapeDtypeStruct(params.shape, jnp.float32),
            jax.ShapeDtypeStruct(params.shape, jnp.bfloat16),
        ],
        scratch_shapes=[
            pltpu.VMEM((steps, unit_rows, width), jnp.float32),
            pltpu.VMEM((steps, unit_rows, width), jnp.bfloat16),
            pltpu.SemaphoreType.DMA((steps,)),
            pltpu.SemaphoreType.DMA((steps,)),
        ],
        input_output_aliases=aliases,
        cost_estimate=pl.CostEstimate(flops=4 * work * V, bytes_accessed=12 * work, transcendentals=0),
        compiler_params=pltpu.CompilerParams(vmem_limit_bytes=24 * 1024 * 1024),
    )(*operands)


def chunk_sizes(own):
    if own <= 4:
        return [own]
    return [own - 4, 4]


def swap(array, axis, distance):
    size = lax.axis_size(axis)
    return lax.ppermute(array, axis, [(i, i ^ distance) for i in range(size)])


def gram_of(rows_array, rows):
    blocks = rows_array.reshape(-1, rows, V)
    return jnp.einsum("mrv,mrw->mvw", blocks, blocks, preferred_element_type=jnp.float32)


def per_device(grads, params, table):
    local = grads[0]
    count, rows, width = local.shape
    replicas = lax.axis_size("dp")
    groups = lax.axis_size("shard")
    members = replicas // CORES
    own = -(-count // members)
    padded = members * own > count
    place = lax.axis_index("dp").astype(jnp.int32)
    core = place % CORES
    member = place // CORES
    if padded:
        filler = jnp.zeros((members * own - count, rows, width), local.dtype)
        local = jnp.concatenate([local, filler], axis=0)
    flat = local.reshape(members * own * rows, width)
    sizes = chunk_sizes(own)

    def rows_of(chip, offset, which, length):
        return lax.dynamic_slice_in_dim(flat, (chip * own + offset) * rows + which * length, length)

    def total_of(terms):
        terms = [term.astype(jnp.float32) for term in terms]
        while len(terms) > 1:
            terms = [sum(terms[i : i + 2][1:], terms[i]) for i in range(0, len(terms), 2)]
        return terms[0]

    def reduce_gram(gram, distance=1):
        while True:
            arrived = swap(gram, "shard", distance)
            distance *= 2
            if distance >= groups:
                return gram, arrived
            gram = gram + arrived

    def over_chips(array):
        return [swap(array, "dp", distance * CORES) for distance in range(1, members)]

    def over_cores(array):
        return [array, swap(array, "dp", 1)]

    def pieces_of(offset, size):
        share = size * rows // CORES
        return [
            rows_of((place ^ distance) // CORES, offset, (place ^ distance) % CORES, share)
            for distance in range(replicas)
        ]

    def exchange(pieces):
        return [swap(piece, "dp", d) if d else piece for d, piece in enumerate(pieces)]

    size = sizes[0]
    terms = exchange(pieces_of(0, size))
    seconds = []
    if len(sizes) > 1:
        pieces = pieces_of(size, sizes[1])
        terms[-1], *pieces = lax.optimization_barrier((terms[-1], *pieces))
        *seconds, late = exchange(pieces)

    first = total_of(terms).astype(jnp.bfloat16)
    whole = size // 2
    if size % 2:
        half = lax.dynamic_slice_in_dim(first, (1 - core) * whole * rows, rows // 2)
        gram = gram_of(half, rows // 2)
        gram = gram + swap(gram, "dp", 1)
        if whole:
            full = lax.dynamic_slice_in_dim(first, core * (rows // 2), whole * rows)
            gram = jnp.concatenate([gram_of(full, rows), gram], axis=0)
    else:
        gram = gram_of(first, rows)
    totals, qs = [first], []
    if seconds:
        *seconds, gram = lax.optimization_barrier((*seconds, gram))
        gram = gram + swap(gram, "shard", 1)
        late, gram = lax.optimization_barrier((late, gram))
        gram = gram + swap(gram, "shard", 2)
        second = total_of([*seconds, late]).astype(jnp.bfloat16)
        totals.append(second)
        gram_second, gram = lax.optimization_barrier((gram_of(second, rows), gram))
        qs.append(newton_schulz(*reduce_gram(gram, 4)))
        pair = reduce_gram(gram_second)
        qs.append(newton_schulz(*pair))
    else:
        qs.append(newton_schulz(*reduce_gram(gram)))

    arrived_q = [over_chips(q) for q in qs]
    arrived_rows = [over_chips(total) for total in totals]
    outputs = []
    for distance in range(members):
        for index, size in enumerate(sizes):
            rows_here, q = totals[index], qs[index]
            if distance:
                tie = qs[-1] if index == len(sizes) - 1 else pair[0]
                rows_here = lax.optimization_barrier((arrived_rows[index][distance - 1], tie))[0]
                q = arrived_q[index][distance - 1]
            per_block = 2 if size % 2 else 1
            units = size * per_block // CORES
            outputs = apply_side(
                [
                    array.reshape(units, rows // per_block, width)
                    for array in over_cores(rows_here)
                ],
                over_cores(q),
                params,
                outputs,
                place.reshape(1),
                table,
                CORES * distance,
                0,
                size,
                sum(sizes[:index]),
                own,
                padded,
            )
            if distance == 0:
                first_q, *outputs = lax.optimization_barrier((arrived_q[index][0], *outputs))
                arrived_q[index][0] = first_q
    new_params, update = outputs
    return (new_params, update)


def solution(mesh):
    return jax.shard_map(
        per_device,
        mesh=mesh,
        in_specs=(P("dp", None, "shard", None), P(None, "shard", None), P()),
        out_specs=(P(None, "shard", None), P(None, "shard", None)),
        check_vma=False,
    )
```

```python
import functools
import math

import jax
import jax.numpy as jnp
from jax import lax
from jax.experimental import pallas as pl
from jax.experimental.pallas import tpu as pltpu
from jax.sharding import PartitionSpec as P

D = 7168
V = 128
ITERS = 5
CORES = 2

quintic_one = 3.4445
quintic_two = -4.775
quintic_three = 2.0315
epsilon = 1e-07
learning_rate = 0.02
decay_rate = 0.1
HIGHEST = lax.Precision.HIGHEST


def dot32(left, right):
    return jnp.dot(left, right, precision=HIGHEST, preferred_element_type=jnp.float32)


def newton_kernel(gram_ref, arrived_ref, *refs):
    *earlier, out_ref = refs
    skip = 0
    for ref in earlier:
        out_ref[: ref.shape[0]] = ref[...]
        skip = ref.shape[0]
    items = gram_ref.shape[0]
    rows = lax.broadcasted_iota(jnp.int32, (V, V), 0)
    columns = lax.broadcasted_iota(jnp.int32, (V, V), 1)
    eye = (rows == columns).astype(jnp.float32)
    grams, scales = [], []
    for item in range(items):
        gram = gram_ref[item] + arrived_ref[item]
        norm_value = jnp.sqrt(jnp.sum(gram * eye))
        scale = 1.0 / (norm_value + epsilon)
        scales.append(scale)
        grams.append((gram * scale) * scale)
    products = [None] * items
    for index in range(ITERS):
        squares = [dot32(gram, gram) for gram in grams]
        polys = [
            quintic_one * eye + quintic_two * gram + quintic_three * square
            for gram, square in zip(grams, squares)
        ]
        if index < ITERS - 1:
            halves = [dot32(gram, poly) for gram, poly in zip(grams, polys)]
        if index == 0:
            products = polys
        else:
            products = [dot32(product, poly) for product, poly in zip(products, polys)]
        if index < ITERS - 1:
            grams = [dot32(half, poly) for half, poly in zip(halves, polys)]
    for item in range(items):
        out_ref[skip + item] = products[item] * scales[item]


def newton_schulz(gram, arrived, *earlier):
    items = gram.shape[0]
    slots = items + sum(q.shape[0] for q in earlier)
    return pl.pallas_call(
        newton_kernel,
        out_shape=jax.ShapeDtypeStruct((slots, V, V), jnp.float32),
        in_specs=[pl.BlockSpec(memory_space=pltpu.VMEM)] * (2 + len(earlier)),
        out_specs=pl.BlockSpec(memory_space=pltpu.VMEM),
        cost_estimate=pl.CostEstimate(
            flops=items * 18 * 12 * V**3, bytes_accessed=items * V * V * 12, transcendentals=0
        ),
        compiler_params=pltpu.CompilerParams(vmem_limit_bytes=16 * 1024 * 1024),
    )(gram, arrived, *earlier)


def apply_kernel(layout, place_ref, table_ref, *refs):
    count, first, base, size, offset, own, total, padded = layout
    sources, qs = refs[:count], refs[count : 2 * count]
    params_ref = refs[2 * count]
    new_ref, update_ref, new_buf, update_buf, new_sems, update_sems = refs[-6:]
    per_block = 2 if size % 2 else 1
    units, unit_rows = sources[0].shape[:2]
    whole = size // 2
    place = place_ref[0]

    def locate(source, unit):
        holder = (place ^ source) & (CORES - 1)
        within = holder * units + unit
        block = within >> (per_block - 1)
        index = ((place ^ source) >> (CORES - 1)) * own + offset + block
        head = table_ref[jnp.minimum(index, total - 1) if padded else index]
        start = pl.multiple_of((within & (per_block - 1)) * unit_rows, unit_rows)
        slot = unit
        if per_block > 1:
            slot = jnp.where(block == whole, whole, block - holder * (whole + 1))
        return index < total, head, pl.ds(start, unit_rows), base + slot

    items = [
        (index, unit, index * units + unit, locate(first + index, unit))
        for index in range(count)
        for unit in range(units)
    ]

    def product(index, unit, slot):
        q = qs[index][slot]
        high = q.astype(jnp.bfloat16)
        low = (q - high.astype(jnp.float32)).astype(jnp.bfloat16)
        rows = sources[index][unit]
        return jnp.dot(
            jnp.concatenate([rows, rows], axis=1),
            jnp.concatenate([high, low], axis=0),
            preferred_element_type=jnp.float32,
        )

    def update(ortho, item, head, span):
        ortho = ortho.astype(jnp.bfloat16).astype(jnp.float32)
        scaled = 0.2 * math.sqrt(max(D, V)) * ortho
        params = params_ref[head, span]
        new_buf[item] = params - learning_rate * (scaled + decay_rate * params)
        update_buf[item] = scaled.astype(jnp.bfloat16)
        pltpu.make_async_copy(new_buf.at[item], new_ref.at[head, span], new_sems.at[item]).start()
        pltpu.make_async_copy(
            update_buf.at[item], update_ref.at[head, span], update_sems.at[item]
        ).start()

    def compute(index, unit, item, head, span, slot):
        update(product(index, unit, slot), item, head, span)

    def finish(item):
        span = pl.ds(0, unit_rows)
        pltpu.make_async_copy(new_buf.at[item], new_ref.at[0, span], new_sems.at[item]).wait()
        pltpu.make_async_copy(
            update_buf.at[item], update_ref.at[0, span], update_sems.at[item]
        ).wait()

    if padded:
        for index, unit, item, (valid, head, span, slot) in items:
            pl.when(valid)(functools.partial(compute, index, unit, item, head, span, slot))
    else:
        products = [product(index, unit, found[3]) for index, unit, _, found in items[:1]]
        for number, (_, _, item, (_, head, span, _)) in enumerate(items):
            for index, unit, _, found in items[number + 1 : number + 2]:
                products.append(product(index, unit, found[3]))
            update(products[number], item, head, span)
    for index, unit, item, (valid, head, span, slot) in items:
        run = functools.partial(finish, item)
        pl.when(valid)(run) if padded else run()


def apply_side(sources, qs, params, previous, place, table, first, base, size, offset, own, padded):
    total, rows, width = params.shape
    count = len(sources)
    units, unit_rows = sources[0].shape[:2]
    steps = count * units
    vmem = pl.BlockSpec(memory_space=pltpu.VMEM)
    hbm = pl.BlockSpec(memory_space=pltpu.HBM)
    smem = pl.BlockSpec(memory_space=pltpu.SMEM)
    operands = [place, table, *sources, *qs, params]
    in_specs = [smem, smem] + [vmem] * (2 * count + 1)
    aliases = {}
    for index, array in enumerate(previous):
        aliases[len(operands)] = index
        operands.append(array)
        in_specs.append(hbm)
    work = steps * unit_rows * width
    layout = (count, first, base, size, offset, own, total, padded)
    return pl.pallas_call(
        functools.partial(apply_kernel, layout),
        in_specs=in_specs,
        out_specs=[hbm, hbm],
        out_shape=[
            jax.ShapeDtypeStruct(params.shape, jnp.float32),
            jax.ShapeDtypeStruct(params.shape, jnp.bfloat16),
        ],
        scratch_shapes=[
            pltpu.VMEM((steps, unit_rows, width), jnp.float32),
            pltpu.VMEM((steps, unit_rows, width), jnp.bfloat16),
            pltpu.SemaphoreType.DMA((steps,)),
            pltpu.SemaphoreType.DMA((steps,)),
        ],
        input_output_aliases=aliases,
        cost_estimate=pl.CostEstimate(flops=4 * work * V, bytes_accessed=12 * work, transcendentals=0),
        compiler_params=pltpu.CompilerParams(vmem_limit_bytes=24 * 1024 * 1024),
    )(*operands)


def chunk_sizes(own):
    if own <= 4:
        return [own]
    return [own - 4, 4]


def swap(array, axis, distance):
    size = lax.axis_size(axis)
    return lax.ppermute(array, axis, [(i, i ^ distance) for i in range(size)])


def gram_of(rows_array, rows):
    blocks = rows_array.reshape(-1, rows, V)
    return jnp.einsum("mrv,mrw->mvw", blocks, blocks, preferred_element_type=jnp.float32)


def per_device(grads, params, table):
    local = grads[0]
    count, rows, width = local.shape
    replicas = lax.axis_size("dp")
    groups = lax.axis_size("shard")
    members = replicas // CORES
    own = -(-count // members)
    padded = members * own > count
    place = lax.axis_index("dp").astype(jnp.int32)
    core = place % CORES
    member = place // CORES
    if padded:
        filler = jnp.zeros((members * own - count, rows, width), local.dtype)
        local = jnp.concatenate([local, filler], axis=0)
    flat = local.reshape(members * own * rows, width)
    sizes = chunk_sizes(own)

    def rows_of(chip, offset, which, length):
        return lax.dynamic_slice_in_dim(flat, (chip * own + offset) * rows + which * length, length)

    def total_of(terms):
        terms = [term.astype(jnp.float32) for term in terms]
        while len(terms) > 1:
            terms = [sum(terms[i : i + 2][1:], terms[i]) for i in range(0, len(terms), 2)]
        return terms[0]

    def reduce_gram(gram, distance=1):
        while True:
            arrived = swap(gram, "shard", distance)
            distance *= 2
            if distance >= groups:
                return gram, arrived
            gram = gram + arrived

    def over_chips(array):
        return [swap(array, "dp", distance * CORES) for distance in range(1, members)]

    def over_cores(array):
        return [array, swap(array, "dp", 1)]

    def pieces_of(offset, size):
        share = size * rows // CORES
        return [
            rows_of((place ^ distance) // CORES, offset, (place ^ distance) % CORES, share)
            for distance in range(replicas)
        ]

    def exchange(pieces):
        return [swap(piece, "dp", d) if d else piece for d, piece in enumerate(pieces)]

    size = sizes[0]
    terms = exchange(pieces_of(0, size))
    seconds = []
    if len(sizes) > 1:
        pieces = pieces_of(size, sizes[1])
        terms[-1], *pieces = lax.optimization_barrier((terms[-1], *pieces))
        *seconds, late = exchange(pieces)

    def apply_one(distance, index, sources, pair_q, outputs):
        size = sizes[index]
        per_block = 2 if size % 2 else 1
        units = size * per_block // CORES
        return apply_side(
            [array.reshape(units, rows // per_block, width) for array in sources],
            pair_q,
            params,
            outputs,
            place.reshape(1),
            table,
            CORES * distance,
            0,
            size,
            sum(sizes[:index]),
            own,
            padded,
        )

    first = total_of(terms).astype(jnp.bfloat16)
    whole = size // 2
    if size % 2:
        half = lax.dynamic_slice_in_dim(first, (1 - core) * whole * rows, rows // 2)
        gram = gram_of(half, rows // 2)
        gram = gram + swap(gram, "dp", 1)
        if whole:
            full = lax.dynamic_slice_in_dim(first, core * (rows // 2), whole * rows)
            gram = jnp.concatenate([gram_of(full, rows), gram], axis=0)
    else:
        gram = gram_of(first, rows)
    totals, qs = [first], []
    if seconds:
        *seconds, gram = lax.optimization_barrier((*seconds, gram))
        gram = gram + swap(gram, "shard", 1)
        late, gram = lax.optimization_barrier((late, gram))
        gram = gram + swap(gram, "shard", 2)
        second = total_of([*seconds, late]).astype(jnp.bfloat16)
        totals.append(second)
        gram_second, gram = lax.optimization_barrier((gram_of(second, rows), gram))
        qs.append(newton_schulz(*reduce_gram(gram, 4)))
        pair = reduce_gram(gram_second)
        outputs = apply_one(0, 0, over_cores(first), over_cores(qs[0]), [])
        pair, outputs = lax.optimization_barrier((pair, list(outputs)))
        qs.append(newton_schulz(*pair))
    else:
        qs.append(newton_schulz(*reduce_gram(gram)))

    arrived_q = [over_chips(q) for q in qs]
    arrived_rows = [over_chips(total) for total in totals]
    if len(sizes) == 1:
        outputs = []
    for distance in range(members):
        for index in range(len(sizes)):
            if distance or index or len(sizes) == 1:
                rows_here, q = totals[index], qs[index]
                if distance:
                    tie = qs[-1] if index == len(sizes) - 1 else pair[0]
                    rows_here = arrived_rows[index][distance - 1]
                    rows_here = lax.optimization_barrier((rows_here, tie))[0]
                    q = arrived_q[index][distance - 1]
                outputs = apply_one(distance, index, over_cores(rows_here), over_cores(q), outputs)
            if distance == 0:
                first_q, *outputs = lax.optimization_barrier((arrived_q[index][0], *outputs))
                arrived_q[index][0] = first_q
    new_params, update = outputs
    return (new_params, update)


def solution(mesh):
    return jax.shard_map(
        per_device,
        mesh=mesh,
        in_specs=(P("dp", None, "shard", None), P(None, "shard", None), P()),
        out_specs=(P(None, "shard", None), P(None, "shard", None)),
        check_vma=False,
    )
```
